32 devices in a mesh: group: 2 (over x), block: 16 (over z, y, core).
Axes of the slice: x: 2, y: 2, z: 4, core: 2. Of those that a mesh axis runs over, the one named last changes fastest.
Arguments:
- block_factor: bfloat16 [4096, 256], P(('group', 'block')), parts along dimension 0, may hold values from 0.0049743652 to 0.049804688
- hour_factor: bfloat16 [16384, 256], P(('group', 'block')), parts along dimension 0, may hold values from 0.0049743652 to 0.049804688
- port_factor: bfloat16 [131072, 256], P(('group', 'block')), parts along dimension 0, may hold values from 0.0049743652 to 0.049804688
- tile_count: int32 [32], P(('group', 'block')), parts along dimension 0, may hold values from 32 to 64, as said below
- hour_tiles: int32 [2048], P(('group', 'block')), parts along dimension 0, may hold values from 0 to 63, as said below
- port_tiles: int32 [2048], P(('group', 'block')), parts along dimension 0, may hold values from 0 to 511, as said below
- entry_coords: int32 [2048, 3, 256], P(('group', 'block')), parts along dimension 0, may hold values from 0 to 127
- entry_counts: int32 [2048, 256], P(('group', 'block')), parts along dimension 0, may hold values from 1 to 8
Outputs:
- block_grad: float32 [4096, 256], P(('group', 'block')), parts along dimension 0
- hour_grad: float32 [16384, 256], P(('group', 'block')), parts along dimension 0
- port_grad: float32 [131072, 256], P(('group', 'block')), parts along dimension 0
The draws below stay inside these ranges and needn't reach their ends.
There are 2 independent parts, one for each index of `group`. The reference program is written for one: setup_inputs(seed, part) draws one part's arguments, and reference() takes and returns one part's arrays. A program takes and returns all parts, laid end to end along the dimension named above; each array names one. Nothing has to cross between parts.
Inputs may be any that keep to these rules, and one draw needn't show every extreme that they name: Each device uses slots 0 to tile_count - 1 of its 64; some device uses all 64. `hour_tiles`: among the 64 slots of one device, live or not, at most 4 name hour tiles whose rows one device holds (device o holds hour tiles o * 4 to o * 4 + 3), and some device reaches 4. `port_tiles`: among the 64 slots of one device, live or not, at most 4 name port tiles whose rows one device holds (device o holds port tiles o * 32 to o * 32 + 31), and some device reaches 4. `entry_coords`: entries of one tile may name the same cell more than once; each is a term of its own.
All inputs are finite; a program needn't handle non-finite values.
Results may differ from the reference program's by a relative error of at most 0.00049.
Values may be sent and summed in bfloat16 or wider, within the bound.
A program may use at most 128 MiB of HBM per device.

```python
import math
import jax
import jax.numpy as jnp
from jax import lax

TILE = 128
RANK = 256
HOURS = 8192
PORTS = 65536
ENT = 256
NT = 64
BLOCKS = 2048
TILES = 1024
HT_DEV = 4
PT_DEV = 32
N_BLOCK = 16


def owner_tiles(key, per_owner):
    keys = jax.random.split(key, N_BLOCK + 1)
    orders = jax.vmap(lambda single: jax.random.permutation(single, N_BLOCK))(keys[:N_BLOCK])
    leading = orders[0]
    first_owner = leading[0]
    leading = jnp.where(leading == N_BLOCK - 1, first_owner, leading)
    leading = jnp.where(jnp.arange(N_BLOCK) == 0, N_BLOCK - 1, leading)
    orders = orders.at[0].set(leading)
    slot_owner = jnp.arange(NT) % N_BLOCK
    owners = orders[:, slot_owner]
    local_tile = jax.random.randint(keys[N_BLOCK], (N_BLOCK, NT), 0, per_owner)
    corner = (jnp.arange(N_BLOCK)[:, None] == 0) & (jnp.arange(NT)[None, :] == 0)
    local_tile = jnp.where(corner, per_owner - 1, local_tile)
    return (owners * per_owner + local_tile).reshape(TILES).astype(jnp.int32)


def draw_tile_count(key, part):
    key = jax.random.fold_in(key, 11)
    first_key, second_key = jax.random.split(key)
    counts = jax.random.randint(first_key, (N_BLOCK,), NT // 2, NT + 1)
    fullest = jax.random.randint(second_key, (), 0, N_BLOCK)
    counts = jnp.where(jnp.arange(N_BLOCK) == fullest, NT, counts)
    return counts.astype(jnp.int32)


def draw_hour_tiles(key, part):
    key = jax.random.fold_in(key, 5)
    return owner_tiles(key, HT_DEV)


def draw_port_tiles(key, part):
    key = jax.random.fold_in(key, 7)
    return owner_tiles(key, PT_DEV)


def place_ends(values, key, smallest, high):
    dims = values.shape
    spot = [jax.random.randint(jax.random.fold_in(key, axis), (), 0, dims[axis]) for axis in range(len(dims))]
    values = values.at[tuple(spot)].set(smallest)
    longest = dims.index(max(dims))
    spot[longest] = (spot[longest] + 1) % dims[longest]
    return values.at[tuple(spot)].set(high)


def level_of(own_key, shape, shards, least, largest):
    level = 1.0
    for position, shards_of in shards:
        heights = jax.random.uniform(jax.random.fold_in(jax.random.fold_in(own_key, 6), position), (shards_of,), jnp.float32, least / len(shards), largest / len(shards))
        level = level * jnp.repeat(jnp.exp(heights), shape[position] // shards_of).reshape((-1,) + (1,) * (len(shape) - 1 - position))
    return level


def setup_inputs(seed: int = 0, part: int = 0) -> dict:
    key_list = jax.random.split(jax.random.key(seed), 9)
    part_keys = jax.random.split(jax.random.fold_in(key_list[8], part), 9)
    block_factor = jnp.clip(jnp.exp(math.log(0.049804688) - 2.3038113 * jax.random.uniform(part_keys[0], (BLOCKS, RANK), jnp.float32) ** level_of(part_keys[0], (BLOCKS, RANK), ((0, 16),), -0.2, 0.2)), 0.0049743652, 0.049804688).astype(jnp.bfloat16)
    hour_factor = jnp.clip(jnp.exp(math.log(0.049804688) - 2.3038113 * jax.random.uniform(part_keys[1], (HOURS, RANK), jnp.float32) ** level_of(part_keys[1], (HOURS, RANK), ((0, 16),), -0.2, 0.2)), 0.0049743652, 0.049804688).astype(jnp.bfloat16)
    port_factor = jnp.clip(jnp.exp(math.log(0.049804688) - 2.3038113 * jax.random.uniform(part_keys[2], (PORTS, RANK), jnp.float32) ** level_of(part_keys[2], (PORTS, RANK), ((0, 16),), -0.2, 0.2)), 0.0049743652, 0.049804688).astype(jnp.bfloat16)
    tile_count = draw_tile_count(jax.random.fold_in(jax.random.fold_in(key_list[8], part), 71), part)
    hour_tiles = draw_hour_tiles(jax.random.fold_in(jax.random.fold_in(key_list[8], part), 71), part)
    port_tiles = draw_port_tiles(jax.random.fold_in(jax.random.fold_in(key_list[8], part), 71), part)
    entry_coords = place_ends(jax.random.randint(part_keys[6], (TILES, 3, ENT), 0, TILE), jax.random.fold_in(part_keys[6], 1), 0, TILE - 1).astype(jnp.int32)
    entry_counts = place_ends(jax.random.randint(part_keys[7], (TILES, ENT), 1, 9), jax.random.fold_in(part_keys[7], 1), 1, 8).astype(jnp.int32)
    return {"block_factor": block_factor, "hour_factor": hour_factor, "port_factor": port_factor, "tile_count": tile_count, "hour_tiles": hour_tiles, "port_tiles": port_tiles, "entry_coords": entry_coords, "entry_counts": entry_counts}


def widen(values):
    narrow = values.astype(jnp.bfloat16)
    narrow = lax.optimization_barrier(narrow)
    return narrow.astype(jnp.float32)


def tile_part(block_rows, hour_rows, port_rows, offsets, counts, live_flag):
    rows_a = jnp.take(block_rows, offsets[0], axis=0).astype(jnp.float32)
    rows_b = jnp.take(hour_rows, offsets[1], axis=0).astype(jnp.float32)
    rows_c = jnp.take(port_rows, offsets[2], axis=0).astype(jnp.float32)
    model = jnp.sum(rows_a * rows_b * rows_c, axis=-1)
    model = jnp.where(live_flag, model, 1.0)
    ratio = jnp.where(live_flag, counts.astype(jnp.float32) / model, 0.0)
    term_a = widen(ratio[:, None] * rows_b * rows_c)
    term_b = widen(ratio[:, None] * rows_a * rows_c)
    term_c = widen(ratio[:, None] * rows_a * rows_b)
    empty = jnp.zeros((TILE, RANK), jnp.float32)
    back_a = empty.at[offsets[0]].add(term_a)
    back_b = empty.at[offsets[1]].add(term_b)
    back_c = empty.at[offsets[2]].add(term_c)
    sum_a = jnp.sum(block_rows.astype(jnp.float32), axis=0)
    sum_b = jnp.sum(hour_rows.astype(jnp.float32), axis=0)
    sum_c = jnp.sum(port_rows.astype(jnp.float32), axis=0)
    weight = live_flag.astype(jnp.float32)
    part_a = weight * (sum_b * sum_c)[None, :] - back_a
    part_b = weight * (sum_a * sum_c)[None, :] - back_b
    part_c = weight * (sum_a * sum_b)[None, :] - back_c
    return part_a, part_b, part_c


def reference(block_factor, hour_factor, port_factor, tile_count, hour_tiles, port_tiles, entry_coords, entry_counts):
    block_stack = block_factor.reshape(N_BLOCK, TILE, RANK)
    hour_stack = hour_factor.reshape(HOURS // TILE, TILE, RANK)
    port_stack = port_factor.reshape(PORTS // TILE, TILE, RANK)

    def visit(carry, slot):
        grad_a, grad_b, grad_c = carry
        owner = (slot // NT).astype(jnp.int32)
        live_flag = (slot % NT) < tile_count[owner]
        hour_index = hour_tiles[slot]
        port_index = port_tiles[slot]
        part_a, part_b, part_c = tile_part(block_stack[owner], hour_stack[hour_index], port_stack[port_index], entry_coords[slot], entry_counts[slot], live_flag)
        grad_a = grad_a.at[owner].add(part_a)
        grad_b = grad_b.at[hour_index].add(part_b)
        grad_c = grad_c.at[port_index].add(part_c)
        return (grad_a, grad_b, grad_c), None

    start = (jnp.zeros((N_BLOCK, TILE, RANK), jnp.float32), jnp.zeros((HOURS // TILE, TILE, RANK), jnp.float32), jnp.zeros((PORTS // TILE, TILE, RANK), jnp.float32))
    final, _ = lax.scan(visit, start, jnp.arange(TILES, dtype=jnp.int32))
    grad_a, grad_b, grad_c = final
    return (grad_a.reshape(BLOCKS, RANK) / TILE, grad_b.reshape(HOURS, RANK) / TILE, grad_c.reshape(PORTS, RANK) / TILE)
```

```python
import functools

import jax
import jax.numpy as jnp
from jax import lax
from jax.experimental import pallas as pl
from jax.experimental.pallas import tpu as pltpu
from jax.sharding import PartitionSpec as P

MESH = pl.DeviceIdType.MESH
PIECES = 2


def ring(devices):
    chips = devices // 2
    half = chips // 2
    me = lax.axis_index("block")
    group = lax.axis_index("group")
    chip = me // 2
    core = me % 2
    odd = chip % 2
    place = (1 - odd) * (chip // 2) + odd * (chips - (chip + 1) // 2)

    def member(offset, lane):
        spot = (place + offset + chips) % chips
        back = spot // half
        at = (1 - back) * (2 * spot) + back * (2 * (chips - spot) - 1)
        return at * 2 + lane

    return group, me, core, member


def greet(group, partners):
    barrier = pltpu.get_barrier_semaphore()
    for partner in partners:
        pl.semaphore_signal(barrier, inc=1, device_id=(group, partner), device_id_type=MESH)
    pl.semaphore_wait(barrier, len(partners))


def gather_kernel(devices, *refs):
    count = (len(refs) - 7) // 2
    ins, outs = refs[:count], refs[count : 2 * count]
    local_sem, send_sem, recv_sem, pair_send, pair_recv, own_send, own_recv = refs[2 * count :]
    reach = devices // 4
    group, me, core, member = ring(devices)
    sibling = member(0, 1 - core)
    greet(group, (member(-1, core), member(1, core), sibling))

    started = []
    for a in range(count):
        keep = pltpu.make_async_copy(ins[a], outs[a].at[me], local_sem.at[a])
        keep.start()
        started.append(keep)

    def hop(a, way, step, piece):
        rows = ins[a].shape[0] // PIECES
        sign = 1 - 2 * way
        origin = member(-sign * (step - 1), core)
        part = pl.ds(piece * rows, rows)
        here = ins[a].at[part] if step == 1 else outs[a].at[origin, part]
        return pltpu.make_async_remote_copy(
            src_ref=here,
            dst_ref=outs[a].at[origin, part],
            send_sem=send_sem.at[a, way, step - 1, piece],
            recv_sem=recv_sem.at[a, way, step - 1, piece],
            device_id=(group, member(sign, core)),
            device_id_type=MESH,
        )

    def share(a, way, step, piece, lane):
        rows = ins[a].shape[0] // PIECES
        sign = 1 - 2 * way
        origin = member(-sign * step, lane)
        part = pl.ds(piece * rows, rows)
        return pltpu.make_async_remote_copy(
            src_ref=outs[a].at[origin, part],
            dst_ref=outs[a].at[origin, part],
            send_sem=pair_send.at[a, way, step - 1, piece],
            recv_sem=pair_recv.at[a, way, step - 1, piece],
            device_id=(group, sibling),
            device_id_type=MESH,
        )

    def own_share(a):
        return pltpu.make_async_remote_copy(
            src_ref=ins[a],
            dst_ref=outs[a].at[me],
            send_sem=own_send.at[a],
            recv_sem=own_recv.at[a],
            device_id=(group, sibling),
            device_id_type=MESH,
        )

    def plan(step):
        pairs = []
        for turn in range(PIECES):
            for way in range(2):
                piece = turn if way == 0 else 1 - turn
                if step < reach or turn == 0:
                    pairs.append((way, piece))
        return pairs

    sends = []
    for way, piece in plan(1):
        for a in range(count):
            copy = hop(a, way, 1, piece)
            copy.start()
            sends.append(copy)
    for a in range(count):
        copy = own_share(a)
        copy.start()
        sends.append(copy)
    for step in range(1, reach + 1):
        onward = plan(step + 1) if step < reach else []
        for way, piece in plan(step):
            for a in range(count):
                hop(a, way, step, piece).wait_recv()
                if (way, piece) in onward:
                    copy = hop(a, way, step + 1, piece)
                    copy.start()
                    sends.append(copy)
                copy = share(a, way, step, piece, core)
                copy.start()
                sends.append(copy)
    for a in range(count):
        own_share(a).wait_recv()
    for step in range(1, reach + 1):
        for way, piece in plan(step):
            for a in range(count):
                share(a, way, step, piece, 1 - core).wait_recv()
    for copy in sends:
        copy.wait_send()
    for copy in started:
        copy.wait()


def gather(devices, *arrays):
    reach = devices // 4
    count = len(arrays)
    sems = (count, 2, reach, PIECES)
    return pl.pallas_call(
        functools.partial(gather_kernel, devices),
        out_shape=[jax.ShapeDtypeStruct((devices,) + x.shape, x.dtype) for x in arrays],
        in_specs=[pl.BlockSpec(memory_space=pl.ANY)] * count,
        out_specs=[pl.BlockSpec(memory_space=pl.ANY)] * count,
        scratch_shapes=[
            pltpu.SemaphoreType.DMA((count,)),
            pltpu.SemaphoreType.DMA(sems),
            pltpu.SemaphoreType.DMA(sems),
            pltpu.SemaphoreType.DMA(sems),
            pltpu.SemaphoreType.DMA(sems),
            pltpu.SemaphoreType.DMA((count,)),
            pltpu.SemaphoreType.DMA((count,)),
        ],
        compiler_params=pltpu.CompilerParams(collective_id=0, has_side_effects=True),
        name="gather_rows",
    )(*arrays)


def scatter_kernel(devices, scale, part, hour_out, block_out, mate, held, *sems):
    send_sem, recv_sem, pair_send, pair_recv = sems
    reach = devices // 4
    chips = devices // 2
    rows = part.shape[1] // PIECES
    group, me, core, member = ring(devices)
    sibling = member(0, 1 - core)
    greet(group, (member(-1, core), member(1, core), sibling))

    def swap(offset):
        return pltpu.make_async_remote_copy(
            src_ref=part.at[member(offset, 1 - core)],
            dst_ref=mate.at[offset % chips],
            send_sem=pair_send.at[offset % chips],
            recv_sem=pair_recv.at[offset % chips],
            device_id=(group, sibling),
            device_id_type=MESH,
        )

    def hop(way, step, piece):
        sign = 1 - 2 * way
        area = pl.ds(piece * rows, rows)
        here = mate.at[reach, area] if step == 1 else held.at[way, step - 2, area]
        return pltpu.make_async_remote_copy(
            src_ref=here,
            dst_ref=held.at[way, step - 1, area],
            send_sem=send_sem.at[way, step - 1, piece],
            recv_sem=recv_sem.at[way, step - 1, piece],
            device_id=(group, member(sign, core)),
            device_id_type=MESH,
        )

    order = [reach]
    for step in range(2, reach + 1):
        order += [reach - step + 1, -(reach - step + 1)]
    order.append(0)
    swaps = [swap(offset) for offset in order]
    for copy in swaps:
        copy.start()
    arrived = {offset: copy for offset, copy in zip(order, swaps)}

    sends = []
    arrived[reach].wait_recv()
    far = member(reach, core)
    for way in range(2):
        area = pl.ds(way * rows, rows)
        mate[reach, area] = mate[reach, area] + part[far, area]
        copy = hop(way, 1, way)
        copy.start()
        sends.append(copy)
    for step in range(2, reach + 1):
        for way in range(2):
            sign = 1 - 2 * way
            offset = sign * (reach - step + 1)
            arrived[offset].wait_recv()
        for turn in range(PIECES):
            for way in range(2):
                sign = 1 - 2 * way
                offset = sign * (reach - step + 1)
                piece = (1 - way if turn == 0 else way) if step == 2 else (1 - way if turn == 0 else way)
                area = pl.ds(piece * rows, rows)
                own = mate[offset % chips, area] + part[member(offset, core), area]
                if step > 2 or piece == way:
                    hop(way, step - 1, piece).wait_recv()
                    own = own + held[way, step - 2, area]
                held[way, step - 2, area] = own
                copy = hop(way, step, piece)
                copy.start()
                sends.append(copy)
    arrived[0].wait_recv()
    for way in range(2):
        for piece in range(PIECES):
            hop(way, reach, piece).wait_recv()
    hours = hour_out.shape[0]
    total = mate[0] + part[me] + held[0, reach - 1] + held[1, reach - 1]
    hour_out[...] = total[:hours] * scale
    block_out[...] = total[hours:] * scale
    for copy in sends:
        copy.wait_send()
    for copy in swaps:
        copy.wait_send()


def scatter(devices, scale, part, hours, blocks):
    reach = devices // 4
    chips = devices // 2
    rows, width = part.shape[1:]
    sems = (2, reach, PIECES)
    return pl.pallas_call(
        functools.partial(scatter_kernel, devices, scale),
        out_shape=[
            jax.ShapeDtypeStruct((hours, width), jnp.float32),
            jax.ShapeDtypeStruct((blocks, width), jnp.float32),
        ],
        in_specs=[pl.BlockSpec(memory_space=pltpu.VMEM)],
        out_specs=[pl.BlockSpec(memory_space=pltpu.VMEM)] * 2,
        scratch_shapes=[
            pltpu.VMEM((chips, rows, width), jnp.float32),
            pltpu.VMEM((2, reach, rows, width), jnp.float32),
            pltpu.SemaphoreType.DMA(sems),
            pltpu.SemaphoreType.DMA(sems),
            pltpu.SemaphoreType.DMA((chips,)),
            pltpu.SemaphoreType.DMA((chips,)),
        ],
        compiler_params=pltpu.CompilerParams(
            collective_id=1, has_side_effects=True, vmem_limit_bytes=56 * 2**20
        ),
        name="scatter_sums",
    )(part)


def tile_kernel(slots, hours, scale, info, total, rows_ref, list_ref, port_ref, part, port_grad):
    side = rows_ref.shape[1] - hours
    width = rows_ref.shape[2]
    entries = list_ref.shape[2]
    per_hour = hours // side
    part[...] = jnp.zeros_like(part)
    port_grad[...] = jnp.zeros_like(port_grad)
    down = lax.broadcasted_iota(jnp.int32, (side, entries), 0)
    along = lax.broadcasted_iota(jnp.int32, (entries, side), 1)

    def visit(step, carry):
        code = info[step]
        flat = code & 0xFFFF
        hour = (code >> 16) & 0xFF
        port = code >> 24
        owner = flat // slots
        slot = flat % slots
        hour_owner = hour // per_hour
        hour_rows = pl.ds(pl.multiple_of((hour % per_hour) * side, side), side)
        port_rows = pl.ds(pl.multiple_of(port * side, side), side)
        first = list_ref[owner, pl.ds(slot, 1), :]
        second = list_ref[owner, pl.ds(slots + slot, 1), :]
        packed = (
            (first & 127)
            + ((first >> 16) << 7)
            + ((second & 127) << 14)
            + ((second >> 16) << 21)
        )
        wide = jnp.broadcast_to(packed, (side, entries))
        tall = wide.T
        put_a = (down == (wide & 127)).astype(jnp.bfloat16)
        put_b = (down == ((wide >> 7) & 127)).astype(jnp.bfloat16)
        put_c = (down == ((wide >> 14) & 127)).astype(jnp.bfloat16)
        pick_a = (along == (tall & 127)).astype(jnp.bfloat16)
        pick_b = (along == ((tall >> 7) & 127)).astype(jnp.bfloat16)
        pick_c = (along == ((tall >> 14) & 127)).astype(jnp.bfloat16)
        counts = (tall >> 21)[:, :1].astype(jnp.float32)
        block_a = rows_ref[owner, pl.ds(hours, side), :]
        block_b = rows_ref[hour_owner, hour_rows, :]
        block_c = port_ref[port_rows, :]
        dot = functools.partial(jnp.dot, preferred_element_type=jnp.float32)
        rows_a = dot(pick_a, block_a)
        rows_b = dot(pick_b, block_b)
        rows_c = dot(pick_c, block_c)
        model = jnp.sum(rows_a * rows_b * rows_c, axis=1, keepdims=True)
        ratio = counts / model
        scaled_a = ratio * rows_a
        scaled_b = ratio * rows_b
        back_a = dot(put_a, (scaled_b * rows_c).astype(jnp.bfloat16))
        back_b = dot(put_b, (scaled_a * rows_c).astype(jnp.bfloat16))
        back_c = dot(put_c, (scaled_a * rows_b).astype(jnp.bfloat16))
        sum_a = jnp.sum(block_a.astype(jnp.float32), axis=0, keepdims=True)
        sum_b = jnp.sum(block_b.astype(jnp.float32), axis=0, keepdims=True)
        sum_c = jnp.sum(block_c.astype(jnp.float32), axis=0, keepdims=True)
        part[owner, pl.ds(hours, side), :] += sum_b * sum_c - back_a
        part[hour_owner, hour_rows, :] += sum_a * sum_c - back_b
        port_grad[port_rows, :] += (sum_a * sum_b - back_c) * scale
        return carry

    lax.fori_loop(0, total[0], visit, 0)


def tiles(slots, hours, scale, info, total, rows, lists, port_factor):
    devices = rows.shape[0]
    vmem = pl.BlockSpec(memory_space=pltpu.VMEM)
    smem = pl.BlockSpec(memory_space=pltpu.SMEM)
    return pl.pallas_call(
        functools.partial(tile_kernel, slots, hours, scale),
        out_shape=[
            jax.ShapeDtypeStruct(rows.shape, jnp.float32),
            jax.ShapeDtypeStruct(port_factor.shape, jnp.float32),
        ],
        in_specs=[smem, smem, vmem, vmem, vmem],
        out_specs=[vmem, vmem],
        compiler_params=pltpu.CompilerParams(vmem_limit_bytes=56 * 2**20),
        name="tile_terms",
    )(info, total, rows, lists, port_factor)


def local(
    block_factor,
    hour_factor,
    port_factor,
    tile_count,
    hour_tiles,
    port_tiles,
    entry_coords,
    entry_counts,
):
    devices = lax.axis_size("block")
    side = block_factor.shape[0]
    hours = hour_factor.shape[0]
    slots = hour_tiles.shape[0]
    entries = entry_counts.shape[1]
    port_local = port_factor.shape[0] // side
    per_peer = (slots + devices - 1) // devices
    capacity = devices * per_peer

    first = entry_coords[:, 0] + (entry_coords[:, 1] << 16)
    second = entry_coords[:, 2] + (entry_counts << 16)
    meta = jnp.stack([hour_tiles, port_tiles, jnp.broadcast_to(tile_count, (slots,))])
    meta = jnp.pad(meta, ((0, 13), (0, entries - slots)))
    rows, lists = gather(
        devices,
        jnp.concatenate([hour_factor, block_factor]),
        jnp.concatenate([first, second, meta]),
    )

    hour_of = lists[:, 2 * slots, :slots]
    port_of = lists[:, 2 * slots + 1, :slots]
    live = jnp.arange(slots, dtype=jnp.int32)[None, :] < lists[:, 2 * slots + 2, :1]
    mine = (live & (port_of // port_local == lax.axis_index("block"))).reshape(-1)
    order = jnp.arange(devices * slots, dtype=jnp.int32)
    code = order + (hour_of.reshape(-1) << 16) + ((port_of % port_local).reshape(-1) << 24)
    before = jnp.sum(
        ((order[None, :] < order[:, None]) & mine[None, :]).astype(jnp.int32), axis=1
    )
    spot = jnp.where(mine, before, capacity)
    hits = spot[None, :] == jnp.arange(capacity, dtype=jnp.int32)[:, None]
    info = jnp.sum(jnp.where(hits, code[None, :], 0), axis=1)
    total = jnp.sum(mine.astype(jnp.int32)).reshape(1)

    scale = 1.0 / side
    part, port_grad = tiles(slots, hours, scale, info, total, rows, lists, port_factor)
    hour_grad, block_grad = scatter(devices, scale, part, hours, side)
    return (block_grad, hour_grad, port_grad)


def solution(mesh):
    row = P(("group", "block"), None)
    one = P(("group", "block"))
    in_specs = (row, row, row, one, one, one, P(("group", "block"), None, None), row)
    return jax.shard_map(
        local, mesh=mesh, in_specs=in_specs, out_specs=(row, row, row), check_vma=False
    )
```

```python
import functools

import jax
import jax.numpy as jnp
from jax import lax
from jax.experimental import pallas as pl
from jax.experimental.pallas import tpu as pltpu
from jax.sharding import PartitionSpec as P

MESH = pl.DeviceIdType.MESH
PIECES = 2
TOGETHER = 2


def ring(devices):
    chips = devices // 2
    half = chips // 2
    me = lax.axis_index("block")
    group = lax.axis_index("group")
    chip = me // 2
    core = me % 2
    odd = chip % 2
    place = (1 - odd) * (chip // 2) + odd * (chips - (chip + 1) // 2)

    def member(offset, lane):
        spot = (place + offset + chips) % chips
        back = spot // half
        at = (1 - back) * (2 * spot) + back * (2 * (chips - spot) - 1)
        return at * 2 + lane

    return group, me, core, member


def greet(group, partners):
    barrier = pltpu.get_barrier_semaphore()
    for partner in partners:
        pl.semaphore_signal(barrier, inc=1, device_id=(group, partner), device_id_type=MESH)
    pl.semaphore_wait(barrier, len(partners))


def file_kernel(port_local, per_peer, tile_count, hour_tiles, port_tiles, coords, counts, box, code, used):
    devices = box.shape[0]
    box[...] = jnp.zeros_like(box)
    code[...] = jnp.full_like(code, -1)

    def clear(owner, carry):
        used[owner] = 0
        return carry

    def visit(slot, carry):
        port = port_tiles[slot]
        owner = port // port_local
        spot = used[owner]
        used[owner] = spot + 1
        word = (hour_tiles[slot] << 16) + port % port_local
        code[owner, pl.ds(spot, 1), :] = jnp.full((1, code.shape[2]), word, jnp.int32)
        at = coords[slot]
        box[owner, pl.ds(2 * spot, 1), :] = at[0:1] + (at[1:2] << 16)
        box[owner, pl.ds(2 * spot + 1, 1), :] = at[2:3] + (counts[pl.ds(slot, 1), :] << 16)
        return carry

    lax.fori_loop(0, devices, clear, 0)
    lax.fori_loop(0, tile_count[0], visit, 0)


def file_lists(devices, port_local, per_peer, tile_count, hour_tiles, port_tiles, coords, counts):
    entries = counts.shape[1]
    vmem = pl.BlockSpec(memory_space=pltpu.VMEM)
    smem = pl.BlockSpec(memory_space=pltpu.SMEM)
    return pl.pallas_call(
        functools.partial(file_kernel, port_local, per_peer),
        out_shape=[
            jax.ShapeDtypeStruct((devices, (2 * per_peer + 7) // 8 * 8, entries), jnp.int32),
            jax.ShapeDtypeStruct((devices, (per_peer + 7) // 8 * 8, 128), jnp.int32),
        ],
        in_specs=[smem, smem, smem, vmem, vmem],
        out_specs=[vmem, vmem],
        scratch_shapes=[pltpu.SMEM((devices,), jnp.int32)],
        name="file_lists",
    )(tile_count, hour_tiles, port_tiles, coords, counts)


def gather_kernel(devices, hour, block, box, code, rows_out, box_out, code_out, *sems):
    (local_sem, send_sem, recv_sem, pair_send, pair_recv, own_send, own_recv, list_send, list_recv) = sems
    ins = (hour, block)
    count = len(ins)
    base = (0, hour.shape[0])
    reach = devices // 4
    group, me, core, member = ring(devices)
    sibling = member(0, 1 - core)
    others = [lax.rem(me + shift, devices) for shift in range(1, devices)]
    greet(group, others)

    def area(a, piece):
        rows = ins[a].shape[0] // PIECES
        return pl.ds(base[a] + piece * rows, rows)

    started = []
    for a in range(count):
        keep = pltpu.make_async_copy(
            ins[a], rows_out.at[me, pl.ds(base[a], ins[a].shape[0])], local_sem.at[a]
        )
        started.append(keep)
    started.append(pltpu.make_async_copy(box.at[me], box_out.at[me], local_sem.at[count]))
    started.append(pltpu.make_async_copy(code.at[me], code_out.at[me], local_sem.at[count + 1]))

    def hop(a, way, step, piece):
        rows = ins[a].shape[0] // PIECES
        sign = 1 - 2 * way
        origin = member(-sign * (step - 1), core)
        there = rows_out.at[origin, area(a, piece)]
        return pltpu.make_async_remote_copy(
            src_ref=ins[a].at[pl.ds(piece * rows, rows)] if step == 1 else there,
            dst_ref=there,
            send_sem=send_sem.at[a, way, step - 1, piece],
            recv_sem=recv_sem.at[a, way, step - 1, piece],
            device_id=(group, member(sign, core)),
            device_id_type=MESH,
        )

    def share(a, way, step, piece, lane):
        sign = 1 - 2 * way
        there = rows_out.at[member(-sign * step, lane), area(a, piece)]
        return pltpu.make_async_remote_copy(
            src_ref=there,
            dst_ref=there,
            send_sem=pair_send.at[a, way, step - 1, piece],
            recv_sem=pair_recv.at[a, way, step - 1, piece],
            device_id=(group, sibling),
            device_id_type=MESH,
        )

    def own_share(a):
        return pltpu.make_async_remote_copy(
            src_ref=ins[a],
            dst_ref=rows_out.at[me, pl.ds(base[a], ins[a].shape[0])],
            send_sem=own_send.at[a],
            recv_sem=own_recv.at[a],
            device_id=(group, sibling),
            device_id_type=MESH,
        )

    def plan(step):
        pairs = []
        for turn in range(PIECES):
            for way in range(2):
                piece = turn if way == 0 else 1 - turn
                if step < reach or turn == 0:
                    pairs.append((way, piece))
        return pairs

    sends = []
    for way, piece in plan(1):
        for a in range(count):
            copy = hop(a, way, 1, piece)
            copy.start()
            sends.append(copy)
    lists = []
    for shift, other in enumerate(others):
        for kind, (here, there) in enumerate(((box, box_out), (code, code_out))):
            copy = pltpu.make_async_remote_copy(
                src_ref=here.at[other],
                dst_ref=there.at[me],
                send_sem=list_send.at[kind, shift],
                recv_sem=list_recv.at[kind, shift],
                device_id=(group, other),
                device_id_type=MESH,
            )
            copy.start()
            lists.append(copy)
    for a in range(count):
        copy = own_share(a)
        copy.start()
        sends.append(copy)
    for keep in started:
        keep.start()
    for step in range(1, reach + 1):
        onward = plan(step + 1) if step < reach else []
        for way, piece in plan(step):
            for a in range(count):
                hop(a, way, step, piece).wait_recv()
                if (way, piece) in onward:
                    copy = hop(a, way, step + 1, piece)
                    copy.start()
                    sends.append(copy)
                copy = share(a, way, step, piece, core)
                copy.start()
                sends.append(copy)
    for copy in lists:
        copy.wait_recv()
    for a in range(count):
        own_share(a).wait_recv()
    for step in range(1, reach + 1):
        for way, piece in plan(step):
            for a in range(count):
                share(a, way, step, piece, 1 - core).wait_recv()
    for copy in sends + lists:
        copy.wait_send()
    for copy in started:
        copy.wait()


def gather(devices, hour, block, box, code):
    reach = devices // 4
    count = 2
    sems = (count, 2, reach, PIECES)
    rows = hour.shape[0] + block.shape[0]
    return pl.pallas_call(
        functools.partial(gather_kernel, devices),
        out_shape=[
            jax.ShapeDtypeStruct((devices, rows, hour.shape[1]), hour.dtype),
            jax.ShapeDtypeStruct(box.shape, box.dtype),
            jax.ShapeDtypeStruct(code.shape, code.dtype),
        ],
        in_specs=[pl.BlockSpec(memory_space=pl.ANY)] * 4,
        out_specs=[pl.BlockSpec(memory_space=pl.ANY)] * 3,
        scratch_shapes=[
            pltpu.SemaphoreType.DMA((count + 2,)),
            pltpu.SemaphoreType.DMA(sems),
            pltpu.SemaphoreType.DMA(sems),
            pltpu.SemaphoreType.DMA(sems),
            pltpu.SemaphoreType.DMA(sems),
            pltpu.SemaphoreType.DMA((count,)),
            pltpu.SemaphoreType.DMA((count,)),
            pltpu.SemaphoreType.DMA((2, devices - 1)),
            pltpu.SemaphoreType.DMA((2, devices - 1)),
        ],
        compiler_params=pltpu.CompilerParams(collective_id=0, has_side_effects=True),
        name="gather_rows",
    )(hour, block, box, code)


def scatter_kernel(devices, scale, part, hour_out, block_out, mate, held, *sems):
    send_sem, recv_sem, pair_send, pair_recv = sems
    reach = devices // 4
    chips = devices // 2
    rows = part.shape[1] // PIECES
    group, me, core, member = ring(devices)
    sibling = member(0, 1 - core)
    greet(group, (member(-1, core), member(1, core), sibling))

    def swap(offset):
        return pltpu.make_async_remote_copy(
            src_ref=part.at[member(offset, 1 - core)],
            dst_ref=mate.at[offset % chips],
            send_sem=pair_send.at[offset % chips],
            recv_sem=pair_recv.at[offset % chips],
            device_id=(group, sibling),
            device_id_type=MESH,
        )

    def hop(way, step, piece):
        sign = 1 - 2 * way
        area = pl.ds(piece * rows, rows)
        here = mate.at[reach, area] if step == 1 else held.at[way, step - 2, area]
        return pltpu.make_async_remote_copy(
            src_ref=here,
            dst_ref=held.at[way, step - 1, area],
            send_sem=send_sem.at[way, step - 1, piece],
            recv_sem=recv_sem.at[way, step - 1, piece],
            device_id=(group, member(sign, core)),
            device_id_type=MESH,
        )

    order = [reach]
    for step in range(2, reach + 1):
        order += [reach - step + 1, -(reach - step + 1)]
    order.append(0)
    swaps = [swap(offset) for offset in order]
    for copy in swaps:
        copy.start()
    arrived = {offset: copy for offset, copy in zip(order, swaps)}

    sends = []
    arrived[reach].wait_recv()
    far = member(reach, core)
    for way in range(2):
        area = pl.ds(way * rows, rows)
        mate[reach, area] = mate[reach, area] + part[far, area]
        copy = hop(way, 1, way)
        copy.start()
        sends.append(copy)
    for step in range(2, reach + 1):
        for way in range(2):
            sign = 1 - 2 * way
            offset = sign * (reach - step + 1)
            arrived[offset].wait_recv()
        for turn in range(PIECES):
            for way in range(2):
                sign = 1 - 2 * way
                offset = sign * (reach - step + 1)
                piece = (1 - way if turn == 0 else way) if step == 2 else (1 - way if turn == 0 else way)
                area = pl.ds(piece * rows, rows)
                own = mate[offset % chips, area] + part[member(offset, core), area]
                if step > 2 or piece == way:
                    hop(way, step - 1, piece).wait_recv()
                    own = own + held[way, step - 2, area]
                held[way, step - 2, area] = own
                copy = hop(way, step, piece)
                copy.start()
                sends.append(copy)
    arrived[0].wait_recv()
    for way in range(2):
        for piece in range(PIECES):
            hop(way, reach, piece).wait_recv()
    hours = hour_out.shape[0]
    total = mate[0] + part[me] + held[0, reach - 1] + held[1, reach - 1]
    hour_out[...] = total[:hours] * scale
    block_out[...] = total[hours:] * scale
    for copy in sends:
        copy.wait_send()
    for copy in swaps:
        copy.wait_send()


def scatter(devices, scale, part, hours, blocks):
    reach = devices // 4
    chips = devices // 2
    rows, width = part.shape[1:]
    sems = (2, reach, PIECES)
    return pl.pallas_call(
        functools.partial(scatter_kernel, devices, scale),
        out_shape=[
            jax.ShapeDtypeStruct((hours, width), jnp.float32),
            jax.ShapeDtypeStruct((blocks, width), jnp.float32),
        ],
        in_specs=[pl.BlockSpec(memory_space=pltpu.VMEM)],
        out_specs=[pl.BlockSpec(memory_space=pltpu.VMEM)] * 2,
        scratch_shapes=[
            pltpu.VMEM((chips, rows, width), jnp.float32),
            pltpu.VMEM((2, reach, rows, width), jnp.float32),
            pltpu.SemaphoreType.DMA(sems),
            pltpu.SemaphoreType.DMA(sems),
            pltpu.SemaphoreType.DMA((chips,)),
            pltpu.SemaphoreType.DMA((chips,)),
        ],
        compiler_params=pltpu.CompilerParams(
            collective_id=1, has_side_effects=True, vmem_limit_bytes=56 * 2**20
        ),
        name="scatter_sums",
    )(part)


def tile_kernel(per_peer, hours, scale, codes, rows_ref, box_ref, port_ref, part, port_grad, kept):
    side = rows_ref.shape[1] - hours
    entries = box_ref.shape[2]
    per_hour = hours // side
    spots = codes.shape[0]

    def keep(spot, count):
        kept[count] = spot
        return count + (codes[spot] >= 0).astype(jnp.int32)

    total = lax.fori_loop(0, spots, keep, 0)
    part[...] = jnp.zeros_like(part)
    port_grad[...] = jnp.zeros_like(port_grad)
    down = lax.broadcasted_iota(jnp.int32, (side, entries), 0)
    along = lax.broadcasted_iota(jnp.int32, (entries, side), 1)
    dot = functools.partial(jnp.dot, preferred_element_type=jnp.float32)

    def terms(index):
        here = index < total
        spot = kept[jnp.minimum(index, total - 1)]
        code = codes[spot]
        hour = code >> 16
        port = code & 0xFFFF
        owner = spot // per_peer
        line = 2 * (spot % per_peer)
        hour_owner = hour // per_hour
        hour_rows = pl.ds(pl.multiple_of((hour % per_hour) * side, side), side)
        port_rows = pl.ds(pl.multiple_of(port * side, side), side)
        first = box_ref[owner, pl.ds(line, 1), :]
        second = box_ref[owner, pl.ds(line + 1, 1), :]
        packed = (
            (first & 127)
            + ((first >> 16) << 7)
            + ((second & 127) << 14)
            + ((second >> 16) << 21)
        )
        wide = jnp.broadcast_to(packed, (side, entries))
        tall = wide.T
        put_a = (down == (wide & 127)).astype(jnp.bfloat16)
        put_b = (down == ((wide >> 7) & 127)).astype(jnp.bfloat16)
        put_c = (down == ((wide >> 14) & 127)).astype(jnp.bfloat16)
        pick_a = (along == (tall & 127)).astype(jnp.bfloat16)
        pick_b = (along == ((tall >> 7) & 127)).astype(jnp.bfloat16)
        pick_c = (along == ((tall >> 14) & 127)).astype(jnp.bfloat16)
        counts = (tall >> 21)[:, :1].astype(jnp.float32)
        block_a = rows_ref[owner, pl.ds(hours, side), :]
        block_b = rows_ref[hour_owner, hour_rows, :]
        block_c = port_ref[port_rows, :]
        rows_a = dot(pick_a, block_a)
        rows_b = dot(pick_b, block_b)
        rows_c = dot(pick_c, block_c)
        model = jnp.sum(rows_a * rows_b * rows_c, axis=1, keepdims=True)
        ratio = jnp.where(here, counts / model, 0.0)
        scaled_a = ratio * rows_a
        scaled_b = ratio * rows_b
        back_a = dot(put_a, (scaled_b * rows_c).astype(jnp.bfloat16))
        back_b = dot(put_b, (scaled_a * rows_c).astype(jnp.bfloat16))
        back_c = dot(put_c, (scaled_a * rows_b).astype(jnp.bfloat16))
        live = jnp.where(here, 1.0, 0.0)
        sum_a = jnp.sum(block_a.astype(jnp.float32), axis=0, keepdims=True)
        sum_b = jnp.sum(block_b.astype(jnp.float32), axis=0, keepdims=True)
        sum_c = jnp.sum(block_c.astype(jnp.float32), axis=0, keepdims=True)
        part_a = live * (sum_b * sum_c) - back_a
        part_b = live * (sum_a * sum_c) - back_b
        part_c = (live * (sum_a * sum_b) - back_c) * scale
        return owner, hour_owner, hour_rows, port_rows, part_a, part_b, part_c

    def visit(step, carry):
        done = [terms(TOGETHER * step + turn) for turn in range(TOGETHER)]
        for owner, hour_owner, hour_rows, port_rows, part_a, part_b, part_c in done:
            part[owner, pl.ds(hours, side), :] += part_a
            part[hour_owner, hour_rows, :] += part_b
            port_grad[port_rows, :] += part_c
        return carry

    lax.fori_loop(0, (total + TOGETHER - 1) // TOGETHER, visit, 0)


def tiles(per_peer, hours, scale, codes, rows, box, port_factor):
    vmem = pl.BlockSpec(memory_space=pltpu.VMEM)
    smem = pl.BlockSpec(memory_space=pltpu.SMEM)
    return pl.pallas_call(
        functools.partial(tile_kernel, per_peer, hours, scale),
        out_shape=[
            jax.ShapeDtypeStruct(rows.shape, jnp.float32),
            jax.ShapeDtypeStruct(port_factor.shape, jnp.float32),
        ],
        in_specs=[smem, vmem, vmem, vmem],
        out_specs=[vmem, vmem],
        scratch_shapes=[pltpu.SMEM((codes.shape[0] + 1,), jnp.int32)],
        compiler_params=pltpu.CompilerParams(vmem_limit_bytes=56 * 2**20),
        name="tile_terms",
    )(codes, rows, box, port_factor)


def local(
    block_factor,
    hour_factor,
    port_factor,
    tile_count,
    hour_tiles,
    port_tiles,
    entry_coords,
    entry_counts,
):
    devices = lax.axis_size("block")
    side = block_factor.shape[0]
    hours = hour_factor.shape[0]
    slots = hour_tiles.shape[0]
    port_local = port_factor.shape[0] // side
    per_peer = (slots + devices - 1) // devices

    box, code = file_lists(
        devices, port_local, per_peer, tile_count, hour_tiles, port_tiles, entry_coords, entry_counts
    )
    rows, box, code = gather(devices, hour_factor, block_factor, box, code)
    codes = code[:, :per_peer, 0].reshape(-1)

    scale = 1.0 / side
    part, port_grad = tiles(per_peer, hours, scale, codes, rows, box, port_factor)
    hour_grad, block_grad = scatter(devices, scale, part, hours, side)
    return (block_grad, hour_grad, port_grad)


def solution(mesh):
    row = P(("group", "block"), None)
    one = P(("group", "block"))
    in_specs = (row, row, row, one, one, one, P(("group", "block"), None, None), row)
    return jax.shard_map(
        local, mesh=mesh, in_specs=in_specs, out_specs=(row, row, row), check_vma=False
    )
```

```python
import functools

import jax
import jax.numpy as jnp
from jax import lax
from jax.experimental import pallas as pl
from jax.experimental.pallas import tpu as pltpu
from jax.sharding import PartitionSpec as P

MESH = pl.DeviceIdType.MESH
PIECES = 2
TOGETHER = 2


def ring(devices):
    chips = devices // 2
    half = chips // 2
    me = lax.axis_index("block")
    group = lax.axis_index("group")
    chip = me // 2
    core = me % 2
    odd = chip % 2
    place = (1 - odd) * (chip // 2) + odd * (chips - (chip + 1) // 2)

    def member(offset, lane):
        spot = (place + offset + chips) % chips
        back = spot // half
        at = (1 - back) * (2 * spot) + back * (2 * (chips - spot) - 1)
        return at * 2 + lane

    return group, me, core, member


def greet(group, partners):
    barrier = pltpu.get_barrier_semaphore()
    for partner in partners:
        pl.semaphore_signal(barrier, inc=1, device_id=(group, partner), device_id_type=MESH)
    pl.semaphore_wait(barrier, len(partners))


def file_kernel(port_local, per_peer, tile_count, hour_tiles, port_tiles, coords, counts, box, code, used):
    devices = box.shape[0]
    box[...] = jnp.zeros_like(box)
    code[...] = jnp.full_like(code, -1)

    def clear(owner, carry):
        used[owner] = 0
        return carry

    def visit(slot, carry):
        port = port_tiles[slot]
        owner = port // port_local
        spot = used[owner]
        used[owner] = spot + 1
        word = (hour_tiles[slot] << 16) + port % port_local
        code[owner, pl.ds(spot, 1), :] = jnp.full((1, code.shape[2]), word, jnp.int32)
        at = coords[slot]
        box[owner, pl.ds(2 * spot, 1), :] = at[0:1] + (at[1:2] << 16)
        box[owner, pl.ds(2 * spot + 1, 1), :] = at[2:3] + (counts[pl.ds(slot, 1), :] << 16)
        return carry

    lax.fori_loop(0, devices, clear, 0)
    lax.fori_loop(0, tile_count[0], visit, 0)


def file_lists(devices, port_local, per_peer, tile_count, hour_tiles, port_tiles, coords, counts):
    entries = counts.shape[1]
    vmem = pl.BlockSpec(memory_space=pltpu.VMEM)
    smem = pl.BlockSpec(memory_space=pltpu.SMEM)
    return pl.pallas_call(
        functools.partial(file_kernel, port_local, per_peer),
        out_shape=[
            jax.ShapeDtypeStruct((devices, (2 * per_peer + 7) // 8 * 8, entries), jnp.int32),
            jax.ShapeDtypeStruct((devices, (per_peer + 7) // 8 * 8, 128), jnp.int32),
        ],
        in_specs=[smem, smem, smem, vmem, vmem],
        out_specs=[vmem, vmem],
        scratch_shapes=[pltpu.SMEM((devices,), jnp.int32)],
        name="file_lists",
    )(tile_count, hour_tiles, port_tiles, coords, counts)


def gather_kernel(devices, hour, block, box, code, rows_out, box_out, code_out, *sems):
    (local_sem, send_sem, recv_sem, pair_send, pair_recv, own_send, own_recv, list_send, list_recv) = sems
    ins = (hour, block)
    count = len(ins)
    base = (0, hour.shape[0])
    reach = devices // 4
    group, me, core, member = ring(devices)
    sibling = member(0, 1 - core)
    others = [lax.rem(me + shift, devices) for shift in range(1, devices)]
    greet(group, others)

    def area(a, piece):
        rows = ins[a].shape[0] // PIECES
        return pl.ds(base[a] + piece * rows, rows)

    started = []
    for a in range(count):
        keep = pltpu.make_async_copy(
            ins[a], rows_out.at[me, pl.ds(base[a], ins[a].shape[0])], local_sem.at[a]
        )
        started.append(keep)
    started.append(pltpu.make_async_copy(box.at[me], box_out.at[me], local_sem.at[count]))
    started.append(pltpu.make_async_copy(code.at[me], code_out.at[me], local_sem.at[count + 1]))

    def hop(a, way, step, piece):
        rows = ins[a].shape[0] // PIECES
        sign = 1 - 2 * way
        origin = member(-sign * (step - 1), core)
        there = rows_out.at[origin, area(a, piece)]
        return pltpu.make_async_remote_copy(
            src_ref=ins[a].at[pl.ds(piece * rows, rows)] if step == 1 else there,
            dst_ref=there,
            send_sem=send_sem.at[a, way, step - 1, piece],
            recv_sem=recv_sem.at[a, way, step - 1, piece],
            device_id=(group, member(sign, core)),
            device_id_type=MESH,
        )

    def share(a, way, step, piece, lane):
        sign = 1 - 2 * way
        there = rows_out.at[member(-sign * step, lane), area(a, piece)]
        return pltpu.make_async_remote_copy(
            src_ref=there,
            dst_ref=there,
            send_sem=pair_send.at[a, way, step - 1, piece],
            recv_sem=pair_recv.at[a, way, step - 1, piece],
            device_id=(group, sibling),
            device_id_type=MESH,
        )

    def own_share(a):
        return pltpu.make_async_remote_copy(
            src_ref=ins[a],
            dst_ref=rows_out.at[me, pl.ds(base[a], ins[a].shape[0])],
            send_sem=own_send.at[a],
            recv_sem=own_recv.at[a],
            device_id=(group, sibling),
            device_id_type=MESH,
        )

    def plan(step):
        pairs = []
        for turn in range(PIECES):
            for way in range(2):
                piece = turn if way == 0 else 1 - turn
                if step < reach or turn == 0:
                    pairs.append((way, piece))
        return pairs

    sends = []
    for way, piece in plan(1):
        for a in range(count):
            copy = hop(a, way, 1, piece)
            copy.start()
            sends.append(copy)
    lists = []
    for shift, other in enumerate(others):
        for kind, (here, there) in enumerate(((box, box_out), (code, code_out))):
            copy = pltpu.make_async_remote_copy(
                src_ref=here.at[other],
                dst_ref=there.at[me],
                send_sem=list_send.at[kind, shift],
                recv_sem=list_recv.at[kind, shift],
                device_id=(group, other),
                device_id_type=MESH,
            )
            copy.start()
            lists.append(copy)
    for a in range(count):
        copy = own_share(a)
        copy.start()
        sends.append(copy)
    for keep in started:
        keep.start()
    for step in range(1, reach + 1):
        onward = plan(step + 1) if step < reach else []
        for way, piece in plan(step):
            for a in range(count):
                hop(a, way, step, piece).wait_recv()
                if (way, piece) in onward:
                    copy = hop(a, way, step + 1, piece)
                    copy.start()
                    sends.append(copy)
                copy = share(a, way, step, piece, core)
                copy.start()
                sends.append(copy)
    for copy in lists:
        copy.wait_recv()
    for a in range(count):
        own_share(a).wait_recv()
    for step in range(1, reach + 1):
        for way, piece in plan(step):
            for a in range(count):
                share(a, way, step, piece, 1 - core).wait_recv()
    for copy in sends + lists:
        copy.wait_send()
    for copy in started:
        copy.wait()


def gather(devices, hour, block, box, code):
    reach = devices // 4
    count = 2
    sems = (count, 2, reach, PIECES)
    rows = hour.shape[0] + block.shape[0]
    return pl.pallas_call(
        functools.partial(gather_kernel, devices),
        out_shape=[
            jax.ShapeDtypeStruct((devices, rows, hour.shape[1]), hour.dtype),
            jax.ShapeDtypeStruct(box.shape, box.dtype),
            jax.ShapeDtypeStruct(code.shape, code.dtype),
        ],
        in_specs=[pl.BlockSpec(memory_space=pl.ANY)] * 4,
        out_specs=[pl.BlockSpec(memory_space=pl.ANY)] * 3,
        scratch_shapes=[
            pltpu.SemaphoreType.DMA((count + 2,)),
            pltpu.SemaphoreType.DMA(sems),
            pltpu.SemaphoreType.DMA(sems),
            pltpu.SemaphoreType.DMA(sems),
            pltpu.SemaphoreType.DMA(sems),
            pltpu.SemaphoreType.DMA((count,)),
            pltpu.SemaphoreType.DMA((count,)),
            pltpu.SemaphoreType.DMA((2, devices - 1)),
            pltpu.SemaphoreType.DMA((2, devices - 1)),
        ],
        compiler_params=pltpu.CompilerParams(collective_id=0, has_side_effects=True),
        name="gather_rows",
    )(hour, block, box, code)


def scatter_kernel(devices, scale, part, hour_out, block_out, mate, held, *sems):
    send_sem, recv_sem, pair_send, pair_recv = sems
    reach = devices // 4
    chips = devices // 2
    rows = part.shape[1] // PIECES
    group, me, core, member = ring(devices)
    sibling = member(0, 1 - core)
    greet(group, (member(-1, core), member(1, core), sibling))

    def swap(offset):
        return pltpu.make_async_remote_copy(
            src_ref=part.at[member(offset, 1 - core)],
            dst_ref=mate.at[offset % chips],
            send_sem=pair_send.at[offset % chips],
            recv_sem=pair_recv.at[offset % chips],
            device_id=(group, sibling),
            device_id_type=MESH,
        )

    def hop(way, step, piece):
        sign = 1 - 2 * way
        area = pl.ds(piece * rows, rows)
        here = mate.at[reach, area] if step == 1 else held.at[way, step - 2, area]
        return pltpu.make_async_remote_copy(
            src_ref=here,
            dst_ref=held.at[way, step - 1, area],
            send_sem=send_sem.at[way, step - 1, piece],
            recv_sem=recv_sem.at[way, step - 1, piece],
            device_id=(group, member(sign, core)),
            device_id_type=MESH,
        )

    order = [reach]
    for step in range(2, reach + 1):
        order += [reach - step + 1, -(reach - step + 1)]
    order.append(0)
    swaps = [swap(offset) for offset in order]
    for copy in swaps:
        copy.start()
    arrived = {offset: copy for offset, copy in zip(order, swaps)}

    sends = []
    arrived[reach].wait_recv()
    far = member(reach, core)
    for way in range(2):
        area = pl.ds(way * rows, rows)
        mate[reach, area] = mate[reach, area] + part[far, area]
        copy = hop(way, 1, way)
        copy.start()
        sends.append(copy)
    for step in range(2, reach + 1):
        for way in range(2):
            sign = 1 - 2 * way
            offset = sign * (reach - step + 1)
            arrived[offset].wait_recv()
        for turn in range(PIECES):
            for way in range(2):
                sign = 1 - 2 * way
                offset = sign * (reach - step + 1)
                piece = (1 - way if turn == 0 else way) if step == 2 else (1 - way if turn == 0 else way)
                area = pl.ds(piece * rows, rows)
                own = mate[offset % chips, area] + part[member(offset, core), area]
                if step > 2 or piece == way:
                    hop(way, step - 1, piece).wait_recv()
                    own = own + held[way, step - 2, area]
                held[way, step - 2, area] = own
                copy = hop(way, step, piece)
                copy.start()
                sends.append(copy)
    arrived[0].wait_recv()
    for way in range(2):
        for piece in range(PIECES):
            hop(way, reach, piece).wait_recv()
    hours = hour_out.shape[0]
    total = mate[0] + part[me] + held[0, reach - 1] + held[1, reach - 1]
    hour_out[...] = total[:hours] * scale
    block_out[...] = total[hours:] * scale
    for copy in sends:
        copy.wait_send()
    for copy in swaps:
        copy.wait_send()


def scatter(devices, scale, part, hours, blocks):
    reach = devices // 4
    chips = devices // 2
    rows, width = part.shape[1:]
    sems = (2, reach, PIECES)
    return pl.pallas_call(
        functools.partial(scatter_kernel, devices, scale),
        out_shape=[
            jax.ShapeDtypeStruct((hours, width), jnp.float32),
            jax.ShapeDtypeStruct((blocks, width), jnp.float32),
        ],
        in_specs=[pl.BlockSpec(memory_space=pltpu.VMEM)],
        out_specs=[pl.BlockSpec(memory_space=pltpu.VMEM)] * 2,
        scratch_shapes=[
            pltpu.VMEM((chips, rows, width), jnp.float32),
            pltpu.VMEM((2, reach, rows, width), jnp.float32),
            pltpu.SemaphoreType.DMA(sems),
            pltpu.SemaphoreType.DMA(sems),
            pltpu.SemaphoreType.DMA((chips,)),
            pltpu.SemaphoreType.DMA((chips,)),
        ],
        compiler_params=pltpu.CompilerParams(
            collective_id=1, has_side_effects=True, vmem_limit_bytes=part.size * 4 + 8 * 2**20
        ),
        name="scatter_sums",
    )(part)


def tile_kernel(per_peer, hours, scale, codes, rows_ref, box_ref, port_ref, part, port_grad, kept):
    side = rows_ref.shape[1] - hours
    entries = box_ref.shape[2]
    per_hour = hours // side
    spots = codes.shape[0]

    def keep(spot, count):
        kept[count] = spot
        return count + (codes[spot] >= 0).astype(jnp.int32)

    total = lax.fori_loop(0, spots, keep, 0)
    part[...] = jnp.zeros_like(part)
    port_grad[...] = jnp.zeros_like(port_grad)
    down = lax.broadcasted_iota(jnp.int32, (side, entries), 0)
    along = lax.broadcasted_iota(jnp.int32, (entries, side), 1)
    dot = functools.partial(jnp.dot, preferred_element_type=jnp.float32)

    def terms(index):
        here = index < total
        spot = kept[jnp.minimum(index, total - 1)]
        code = codes[spot]
        hour = code >> 16
        port = code & 0xFFFF
        owner = spot // per_peer
        line = 2 * (spot % per_peer)
        hour_owner = hour // per_hour
        hour_rows = pl.ds(pl.multiple_of((hour % per_hour) * side, side), side)
        port_rows = pl.ds(pl.multiple_of(port * side, side), side)
        first = box_ref[owner, pl.ds(line, 1), :]
        second = box_ref[owner, pl.ds(line + 1, 1), :]
        packed = (
            (first & 127)
            + ((first >> 16) << 7)
            + ((second & 127) << 14)
            + ((second >> 16) << 21)
        )
        wide = jnp.broadcast_to(packed, (side, entries))
        tall = wide.T
        put_a = (down == (first & 127)).astype(jnp.bfloat16)
        put_b = (down == (first >> 16)).astype(jnp.bfloat16)
        put_c = (down == (second & 127)).astype(jnp.bfloat16)
        pick_a = (along == (tall & 127)).astype(jnp.bfloat16)
        pick_b = ((along << 7) == (tall & (127 << 7))).astype(jnp.bfloat16)
        pick_c = ((along << 14) == (tall & (127 << 14))).astype(jnp.bfloat16)
        counts = (tall >> 21)[:, :1].astype(jnp.float32)
        block_a = rows_ref[owner, pl.ds(hours, side), :]
        block_b = rows_ref[hour_owner, hour_rows, :]
        block_c = port_ref[port_rows, :]
        rows_a = dot(pick_a, block_a)
        rows_b = dot(pick_b, block_b)
        rows_c = dot(pick_c, block_c)
        model = jnp.sum(rows_a * rows_b * rows_c, axis=1, keepdims=True)
        ratio = jnp.where(here, counts / model, 0.0)
        scaled_a = ratio * rows_a
        scaled_b = ratio * rows_b
        back_a = dot(put_a, (scaled_b * rows_c).astype(jnp.bfloat16))
        back_b = dot(put_b, (scaled_a * rows_c).astype(jnp.bfloat16))
        back_c = dot(put_c, (scaled_a * rows_b).astype(jnp.bfloat16))
        live = jnp.where(here, 1.0, 0.0)
        sum_a = jnp.sum(block_a.astype(jnp.float32), axis=0, keepdims=True)
        sum_b = jnp.sum(block_b.astype(jnp.float32), axis=0, keepdims=True)
        sum_c = jnp.sum(block_c.astype(jnp.float32), axis=0, keepdims=True)
        part_a = live * (sum_b * sum_c) - back_a
        part_b = live * (sum_a * sum_c) - back_b
        part_c = (live * (sum_a * sum_b) - back_c) * scale
        return owner, hour_owner, hour_rows, port_rows, part_a, part_b, part_c

    def visit(step, carry):
        done = [terms(TOGETHER * step + turn) for turn in range(TOGETHER)]
        for owner, hour_owner, hour_rows, port_rows, part_a, part_b, part_c in done:
            part[owner, pl.ds(hours, side), :] += part_a
            part[hour_owner, hour_rows, :] += part_b
            port_grad[port_rows, :] += part_c
        return carry

    lax.fori_loop(0, (total + TOGETHER - 1) // TOGETHER, visit, 0)


def tiles(per_peer, hours, scale, codes, rows, box, port_factor):
    vmem = pl.BlockSpec(memory_space=pltpu.VMEM)
    smem = pl.BlockSpec(memory_space=pltpu.SMEM)
    return pl.pallas_call(
        functools.partial(tile_kernel, per_peer, hours, scale),
        out_shape=[
            pltpu.VMEM(rows.shape, jnp.float32),
            jax.ShapeDtypeStruct(port_factor.shape, jnp.float32),
        ],
        in_specs=[smem, vmem, vmem, vmem],
        out_specs=[vmem, vmem],
        scratch_shapes=[pltpu.SMEM((codes.shape[0] + 1,), jnp.int32)],
        compiler_params=pltpu.CompilerParams(
            vmem_limit_bytes=rows.size * 2 + port_factor.size * 6 + 8 * 2**20
        ),
        name="tile_terms",
    )(codes, rows, box, port_factor)


def local(
    block_factor,
    hour_factor,
    port_factor,
    tile_count,
    hour_tiles,
    port_tiles,
    entry_coords,
    entry_counts,
):
    devices = lax.axis_size("block")
    side = block_factor.shape[0]
    hours = hour_factor.shape[0]
    slots = hour_tiles.shape[0]
    port_local = port_factor.shape[0] // side
    per_peer = (slots + devices - 1) // devices

    box, code = file_lists(
        devices, port_local, per_peer, tile_count, hour_tiles, port_tiles, entry_coords, entry_counts
    )
    rows, box, code = gather(devices, hour_factor, block_factor, box, code)
    codes = code[:, :per_peer, 0].reshape(-1)

    scale = 1.0 / side
    part, port_grad = tiles(per_peer, hours, scale, codes, rows, box, port_factor)
    hour_grad, block_grad = scatter(devices, scale, part, hours, side)
    return (block_grad, hour_grad, port_grad)


def solution(mesh):
    row = P(("group", "block"), None)
    one = P(("group", "block"))
    in_specs = (row, row, row, one, one, one, P(("group", "block"), None, None), row)
    return jax.shard_map(
        local, mesh=mesh, in_specs=in_specs, out_specs=(row, row, row), check_vma=False
    )
```

```python
import functools

import jax
import jax.numpy as jnp
from jax import lax
from jax.experimental import pallas as pl
from jax.experimental.pallas import tpu as pltpu
from jax.sharding import PartitionSpec as P

MESH = pl.DeviceIdType.MESH
PIECES = 2
TOGETHER = 2


def ring(devices):
    chips = devices // 2
    half = chips // 2
    me = lax.axis_index("block")
    group = lax.axis_index("group")
    chip = me // 2
    core = me % 2
    odd = chip % 2
    place = (1 - odd) * (chip // 2) + odd * (chips - (chip + 1) // 2)

    def member(offset, lane):
        spot = (place + offset + chips) % chips
        back = spot // half
        at = (1 - back) * (2 * spot) + back * (2 * (chips - spot) - 1)
        return at * 2 + lane

    return group, me, core, member


def greet(group, partners):
    barrier = pltpu.get_barrier_semaphore()
    for partner in partners:
        pl.semaphore_signal(barrier, inc=1, device_id=(group, partner), device_id_type=MESH)
    pl.semaphore_wait(barrier, len(partners))


def file_kernel(port_local, per_peer, tile_count, hour_tiles, port_tiles, coords, counts, box, code, used):
    devices = box.shape[0]
    box[...] = jnp.zeros_like(box)
    code[...] = jnp.full_like(code, -1)

    def clear(owner, carry):
        used[owner] = 0
        return carry

    def visit(slot, carry):
        port = port_tiles[slot]
        owner = port // port_local
        spot = used[owner]
        used[owner] = spot + 1
        word = (hour_tiles[slot] << 16) + port % port_local
        code[owner, pl.ds(spot, 1), :] = jnp.full((1, code.shape[2]), word, jnp.int32)
        at = coords[slot]
        box[owner, pl.ds(2 * spot, 1), :] = at[0:1] + (at[1:2] << 16)
        box[owner, pl.ds(2 * spot + 1, 1), :] = at[2:3] + (counts[pl.ds(slot, 1), :] << 16)
        return carry

    lax.fori_loop(0, devices, clear, 0)
    lax.fori_loop(0, tile_count[0], visit, 0)


def file_lists(devices, port_local, per_peer, tile_count, hour_tiles, port_tiles, coords, counts):
    entries = counts.shape[1]
    vmem = pl.BlockSpec(memory_space=pltpu.VMEM)
    smem = pl.BlockSpec(memory_space=pltpu.SMEM)
    return pl.pallas_call(
        functools.partial(file_kernel, port_local, per_peer),
        out_shape=[
            jax.ShapeDtypeStruct((devices, (2 * per_peer + 7) // 8 * 8, entries), jnp.int32),
            jax.ShapeDtypeStruct((devices, (per_peer + 7) // 8 * 8, 128), jnp.int32),
        ],
        in_specs=[smem, smem, smem, vmem, vmem],
        out_specs=[vmem, vmem],
        scratch_shapes=[pltpu.SMEM((devices,), jnp.int32)],
        name="file_lists",
    )(tile_count, hour_tiles, port_tiles, coords, counts)


def gather_kernel(devices, hour, block, box, code, rows_out, box_out, code_out, *sems):
    (local_sem, send_sem, recv_sem, pair_send, pair_recv, own_send, own_recv, list_send, list_recv) = sems
    ins = (hour, block)
    count = len(ins)
    base = (0, hour.shape[0])
    reach = devices // 4
    group, me, core, member = ring(devices)
    sibling = member(0, 1 - core)
    others = [lax.rem(me + shift, devices) for shift in range(1, devices)]
    greet(group, others)

    def area(a, piece):
        rows = ins[a].shape[0] // PIECES
        return pl.ds(base[a] + piece * rows, rows)

    started = []
    for a in range(count):
        keep = pltpu.make_async_copy(
            ins[a], rows_out.at[me, pl.ds(base[a], ins[a].shape[0])], local_sem.at[a]
        )
        started.append(keep)
    started.append(pltpu.make_async_copy(box.at[me], box_out.at[me], local_sem.at[count]))
    started.append(pltpu.make_async_copy(code.at[me], code_out.at[me], local_sem.at[count + 1]))

    def hop(a, way, step, piece):
        rows = ins[a].shape[0] // PIECES
        sign = 1 - 2 * way
        origin = member(-sign * (step - 1), core)
        there = rows_out.at[origin, area(a, piece)]
        return pltpu.make_async_remote_copy(
            src_ref=ins[a].at[pl.ds(piece * rows, rows)] if step == 1 else there,
            dst_ref=there,
            send_sem=send_sem.at[a, way, step - 1, piece],
            recv_sem=recv_sem.at[a, way, step - 1, piece],
            device_id=(group, member(sign, core)),
            device_id_type=MESH,
        )

    def share(a, way, step, piece, lane):
        sign = 1 - 2 * way
        there = rows_out.at[member(-sign * step, lane), area(a, piece)]
        return pltpu.make_async_remote_copy(
            src_ref=there,
            dst_ref=there,
            send_sem=pair_send.at[a, way, step - 1, piece],
            recv_sem=pair_recv.at[a, way, step - 1, piece],
            device_id=(group, sibling),
            device_id_type=MESH,
        )

    def own_share(a):
        return pltpu.make_async_remote_copy(
            src_ref=ins[a],
            dst_ref=rows_out.at[me, pl.ds(base[a], ins[a].shape[0])],
            send_sem=own_send.at[a],
            recv_sem=own_recv.at[a],
            device_id=(group, sibling),
            device_id_type=MESH,
        )

    def plan(step):
        pairs = []
        for turn in range(PIECES):
            for way in range(2):
                piece = turn if way == 0 else 1 - turn
                if step < reach or turn == 0:
                    pairs.append((way, piece))
        return pairs

    sends = []
    for way, piece in plan(1):
        for a in range(count):
            copy = hop(a, way, 1, piece)
            copy.start()
            sends.append(copy)
    lists = []
    for shift, other in enumerate(others):
        for kind, (here, there) in enumerate(((box, box_out), (code, code_out))):
            copy = pltpu.make_async_remote_copy(
                src_ref=here.at[other],
                dst_ref=there.at[me],
                send_sem=list_send.at[kind, shift],
                recv_sem=list_recv.at[kind, shift],
                device_id=(group, other),
                device_id_type=MESH,
            )
            copy.start()
            lists.append(copy)
    for a in range(count):
        copy = own_share(a)
        copy.start()
        sends.append(copy)
    for keep in started:
        keep.start()
    for step in range(1, reach + 1):
        onward = plan(step + 1) if step < reach else []
        for way, piece in plan(step):
            for a in range(count):
                hop(a, way, step, piece).wait_recv()
                if (way, piece) in onward:
                    copy = hop(a, way, step + 1, piece)
                    copy.start()
                    sends.append(copy)
                copy = share(a, way, step, piece, core)
                copy.start()
                sends.append(copy)
    for copy in lists:
        copy.wait_recv()
    for a in range(count):
        own_share(a).wait_recv()
    for step in range(1, reach + 1):
        for way, piece in plan(step):
            for a in range(count):
                share(a, way, step, piece, 1 - core).wait_recv()
    for copy in sends + lists:
        copy.wait_send()
    for copy in started:
        copy.wait()


def gather(devices, hour, block, box, code):
    reach = devices // 4
    count = 2
    sems = (count, 2, reach, PIECES)
    rows = hour.shape[0] + block.shape[0]
    return pl.pallas_call(
        functools.partial(gather_kernel, devices),
        out_shape=[
            pltpu.VMEM((devices, rows, hour.shape[1]), hour.dtype),
            pltpu.VMEM(box.shape, box.dtype),
            jax.ShapeDtypeStruct(code.shape, code.dtype),
        ],
        in_specs=[pl.BlockSpec(memory_space=pl.ANY)] * 4,
        out_specs=[pl.BlockSpec(memory_space=pltpu.VMEM)] * 2 + [pl.BlockSpec(memory_space=pl.ANY)],
        scratch_shapes=[
            pltpu.SemaphoreType.DMA((count + 2,)),
            pltpu.SemaphoreType.DMA(sems),
            pltpu.SemaphoreType.DMA(sems),
            pltpu.SemaphoreType.DMA(sems),
            pltpu.SemaphoreType.DMA(sems),
            pltpu.SemaphoreType.DMA((count,)),
            pltpu.SemaphoreType.DMA((count,)),
            pltpu.SemaphoreType.DMA((2, devices - 1)),
            pltpu.SemaphoreType.DMA((2, devices - 1)),
        ],
        compiler_params=pltpu.CompilerParams(
            collective_id=0, has_side_effects=True, vmem_limit_bytes=8 * 2**20
        ),
        name="gather_rows",
    )(hour, block, box, code)


def scatter_kernel(devices, scale, part, hour_out, block_out, mate, held, *sems):
    send_sem, recv_sem, pair_send, pair_recv = sems
    reach = devices // 4
    chips = devices // 2
    rows = part.shape[1] // PIECES
    group, me, core, member = ring(devices)
    sibling = member(0, 1 - core)
    greet(group, (member(-1, core), member(1, core), sibling))

    def swap(offset):
        return pltpu.make_async_remote_copy(
            src_ref=part.at[member(offset, 1 - core)],
            dst_ref=mate.at[offset % chips],
            send_sem=pair_send.at[offset % chips],
            recv_sem=pair_recv.at[offset % chips],
            device_id=(group, sibling),
            device_id_type=MESH,
        )

    def hop(way, step, piece):
        sign = 1 - 2 * way
        area = pl.ds(piece * rows, rows)
        here = mate.at[reach, area] if step == 1 else held.at[way, step - 2, area]
        return pltpu.make_async_remote_copy(
            src_ref=here,
            dst_ref=held.at[way, step - 1, area],
            send_sem=send_sem.at[way, step - 1, piece],
            recv_sem=recv_sem.at[way, step - 1, piece],
            device_id=(group, member(sign, core)),
            device_id_type=MESH,
        )

    order = [reach]
    for step in range(2, reach + 1):
        order += [reach - step + 1, -(reach - step + 1)]
    order.append(0)
    swaps = [swap(offset) for offset in order]
    for copy in swaps:
        copy.start()
    arrived = {offset: copy for offset, copy in zip(order, swaps)}

    sends = []
    arrived[reach].wait_recv()
    far = member(reach, core)
    for way in range(2):
        area = pl.ds(way * rows, rows)
        mate[reach, area] = mate[reach, area] + part[far, area]
        copy = hop(way, 1, way)
        copy.start()
        sends.append(copy)
    for step in range(2, reach + 1):
        for way in range(2):
            sign = 1 - 2 * way
            offset = sign * (reach - step + 1)
            arrived[offset].wait_recv()
        for turn in range(PIECES):
            for way in range(2):
                sign = 1 - 2 * way
                offset = sign * (reach - step + 1)
                piece = (1 - way if turn == 0 else way) if step == 2 else (1 - way if turn == 0 else way)
                area = pl.ds(piece * rows, rows)
                own = mate[offset % chips, area] + part[member(offset, core), area]
                if step > 2 or piece == way:
                    hop(way, step - 1, piece).wait_recv()
                    own = own + held[way, step - 2, area]
                held[way, step - 2, area] = own
                copy = hop(way, step, piece)
                copy.start()
                sends.append(copy)
    arrived[0].wait_recv()
    for way in range(2):
        for piece in range(PIECES):
            hop(way, reach, piece).wait_recv()
    hours = hour_out.shape[0]
    total = mate[0] + part[me] + held[0, reach - 1] + held[1, reach - 1]
    hour_out[...] = total[:hours] * scale
    block_out[...] = total[hours:] * scale
    for copy in sends:
        copy.wait_send()
    for copy in swaps:
        copy.wait_send()


def scatter(devices, scale, part, hours, blocks):
    reach = devices // 4
    chips = devices // 2
    rows, width = part.shape[1:]
    sems = (2, reach, PIECES)
    return pl.pallas_call(
        functools.partial(scatter_kernel, devices, scale),
        out_shape=[
            jax.ShapeDtypeStruct((hours, width), jnp.float32),
            jax.ShapeDtypeStruct((blocks, width), jnp.float32),
        ],
        in_specs=[pl.BlockSpec(memory_space=pltpu.VMEM)],
        out_specs=[pl.BlockSpec(memory_space=pltpu.VMEM)] * 2,
        scratch_shapes=[
            pltpu.VMEM((chips, rows, width), jnp.float32),
            pltpu.VMEM((2, reach, rows, width), jnp.float32),
            pltpu.SemaphoreType.DMA(sems),
            pltpu.SemaphoreType.DMA(sems),
            pltpu.SemaphoreType.DMA((chips,)),
            pltpu.SemaphoreType.DMA((chips,)),
        ],
        compiler_params=pltpu.CompilerParams(
            collective_id=1, has_side_effects=True, vmem_limit_bytes=part.size * 4 + 8 * 2**20
        ),
        name="scatter_sums",
    )(part)


def tile_kernel(per_peer, hours, scale, codes, rows_ref, box_ref, port_ref, part, port_grad, kept):
    side = rows_ref.shape[1] - hours
    entries = box_ref.shape[2]
    per_hour = hours // side
    spots = codes.shape[0]

    def keep(spot, count):
        kept[count] = spot
        return count + (codes[spot] >= 0).astype(jnp.int32)

    total = lax.fori_loop(0, spots, keep, 0)
    part[...] = jnp.zeros_like(part)
    port_grad[...] = jnp.zeros_like(port_grad)
    down = lax.broadcasted_iota(jnp.int32, (side, entries), 0)
    along = lax.broadcasted_iota(jnp.int32, (entries, side), 1)
    dot = functools.partial(jnp.dot, preferred_element_type=jnp.float32)

    def terms(index):
        here = index < total
        spot = kept[jnp.minimum(index, total - 1)]
        code = codes[spot]
        hour = code >> 16
        port = code & 0xFFFF
        owner = spot // per_peer
        line = 2 * (spot % per_peer)
        hour_owner = hour // per_hour
        hour_rows = pl.ds(pl.multiple_of((hour % per_hour) * side, side), side)
        port_rows = pl.ds(pl.multiple_of(port * side, side), side)
        first = box_ref[owner, pl.ds(line, 1), :]
        second = box_ref[owner, pl.ds(line + 1, 1), :]
        packed = (
            (first & 127)
            + ((first >> 16) << 7)
            + ((second & 127) << 14)
            + ((second >> 16) << 21)
        )
        wide = jnp.broadcast_to(packed, (side, entries))
        tall = wide.T
        put_a = (down == (first & 127)).astype(jnp.bfloat16)
        put_b = (down == (first >> 16)).astype(jnp.bfloat16)
        put_c = (down == (second & 127)).astype(jnp.bfloat16)
        pick_a = (along == (tall & 127)).astype(jnp.bfloat16)
        pick_b = ((along << 7) == (tall & (127 << 7))).astype(jnp.bfloat16)
        pick_c = ((along << 14) == (tall & (127 << 14))).astype(jnp.bfloat16)
        counts = (tall >> 21)[:, :1].astype(jnp.float32)
        block_a = rows_ref[owner, pl.ds(hours, side), :]
        block_b = rows_ref[hour_owner, hour_rows, :]
        block_c = port_ref[port_rows, :]
        rows_a = dot(pick_a, block_a)
        rows_b = dot(pick_b, block_b)
        rows_c = dot(pick_c, block_c)
        model = jnp.sum(rows_a * rows_b * rows_c, axis=1, keepdims=True)
        ratio = jnp.where(here, counts / model, 0.0)
        scaled_a = ratio * rows_a
        scaled_b = ratio * rows_b
        back_a = dot(put_a, (scaled_b * rows_c).astype(jnp.bfloat16))
        back_b = dot(put_b, (scaled_a * rows_c).astype(jnp.bfloat16))
        back_c = dot(put_c, (scaled_a * rows_b).astype(jnp.bfloat16))
        live = jnp.where(here, 1.0, 0.0)
        sum_a = jnp.sum(block_a.astype(jnp.float32), axis=0, keepdims=True)
        sum_b = jnp.sum(block_b.astype(jnp.float32), axis=0, keepdims=True)
        sum_c = jnp.sum(block_c.astype(jnp.float32), axis=0, keepdims=True)
        part_a = live * (sum_b * sum_c) - back_a
        part_b = live * (sum_a * sum_c) - back_b
        part_c = (live * (sum_a * sum_b) - back_c) * scale
        return owner, hour_owner, hour_rows, port_rows, part_a, part_b, part_c

    def visit(step, carry):
        done = [terms(TOGETHER * step + turn) for turn in range(TOGETHER)]
        for owner, hour_owner, hour_rows, port_rows, part_a, part_b, part_c in done:
            part[owner, pl.ds(hours, side), :] += part_a
            part[hour_owner, hour_rows, :] += part_b
            port_grad[port_rows, :] += part_c
        return carry

    lax.fori_loop(0, (total + TOGETHER - 1) // TOGETHER, visit, 0)


def tiles(per_peer, hours, scale, codes, rows, box, port_factor):
    vmem = pl.BlockSpec(memory_space=pltpu.VMEM)
    smem = pl.BlockSpec(memory_space=pltpu.SMEM)
    return pl.pallas_call(
        functools.partial(tile_kernel, per_peer, hours, scale),
        out_shape=[
            pltpu.VMEM(rows.shape, jnp.float32),
            jax.ShapeDtypeStruct(port_factor.shape, jnp.float32),
        ],
        in_specs=[smem, vmem, vmem, vmem],
        out_specs=[vmem, vmem],
        scratch_shapes=[pltpu.SMEM((codes.shape[0] + 1,), jnp.int32)],
        compiler_params=pltpu.CompilerParams(
            vmem_limit_bytes=rows.size * 2 + port_factor.size * 6 + 8 * 2**20
        ),
        name="tile_terms",
    )(codes, rows, box, port_factor)


def local(
    block_factor,
    hour_factor,
    port_factor,
    tile_count,
    hour_tiles,
    port_tiles,
    entry_coords,
    entry_counts,
):
    devices = lax.axis_size("block")
    side = block_factor.shape[0]
    hours = hour_factor.shape[0]
    slots = hour_tiles.shape[0]
    port_local = port_factor.shape[0] // side
    per_peer = (slots + devices - 1) // devices

    box, code = file_lists(
        devices, port_local, per_peer, tile_count, hour_tiles, port_tiles, entry_coords, entry_counts
    )
    rows, box, code = gather(devices, hour_factor, block_factor, box, code)
    codes = code[:, :per_peer, 0].reshape(-1)

    scale = 1.0 / side
    part, port_grad = tiles(per_peer, hours, scale, codes, rows, box, port_factor)
    hour_grad, block_grad = scatter(devices, scale, part, hours, side)
    return (block_grad, hour_grad, port_grad)


def solution(mesh):
    row = P(("group", "block"), None)
    one = P(("group", "block"))
    in_specs = (row, row, row, one, one, one, P(("group", "block"), None, None), row)
    return jax.shard_map(
        local, mesh=mesh, in_specs=in_specs, out_specs=(row, row, row), check_vma=False
    )
```
